32 devices in a mesh: row: 16 (over z, y, core), off: 2 (over x).
Axes of the slice: x: 2, y: 2, z: 4, core: 2. Of those that a mesh axis runs over, the one named last changes fastest.
Arguments:
- vectors: float32 [16384, 128], P(('row', 'off')), may hold values from -6 to 6
- blocks: float32 [16, 2, 48, 128, 128], P('row', 'off'), may hold values from -0.125 to 0.125
- lists: int32 [16, 2, 2, 48], P('row', 'off'), may hold values from 0 to 7, as said below
Outputs:
- filtered: float32 [16384, 128], P(('row', 'off'))
The draws below stay inside these ranges and needn't reach their ends.
Inputs may be any that keep to these rules, and one draw needn't show every extreme that they name: `lists`: within each tile the 48 listed blocks are distinct positions of its 8 x 8 grid of blocks.
All inputs are finite; a program needn't handle non-finite values.
Results may differ from the reference program's by a relative error of at most 0.00011.
Values sent between devices are 32-bit elements; how exact they have to be, the bound alone decides.
No kernel may reach another device: no remote copies, remote signals or barrier semaphores. Data moves between devices by JAX's collectives and lax.ppermute only.
A program may use at most 64 MiB of HBM per device.

```python
import jax
import jax.numpy as jnp
from jax import lax

TILE = 1024
BS = 128
NV = 128
DEGREE = 4
TB = 8
NBLK = 48
ROW_BLOCKS = 16
OFFSETS = 2
STATES = 16384
N_OFF = 2


def draw_lists(key, part):
    key_list = jax.random.split(jax.random.fold_in(key, 17), ROW_BLOCKS * OFFSETS)

    def one_tile(tile_key):
        return jax.random.permutation(tile_key, TB * TB)[:NBLK]
    chosen = jax.vmap(one_tile)(key_list).astype(jnp.int32)
    chosen = chosen.reshape(ROW_BLOCKS, OFFSETS, NBLK)
    return jnp.stack([chosen // TB, chosen % TB], axis=2).astype(jnp.int32)


def block_scale(key, extent, pieces, least, top_value):
    gain, own = 1.0, jax.random.fold_in(key, 6)
    for dim, blocks in pieces:
        heights = jnp.exp(jax.random.uniform(jax.random.fold_in(own, dim), (blocks,), jnp.float32, least / len(pieces), top_value / len(pieces)))
        gain = gain * jnp.repeat(heights, extent[dim] // blocks).reshape([-1 if axis == dim else 1 for axis in range(len(extent))])
    return gain


def bell_draw(stream_key, extent, spread, bound, cuts=(), kind=jnp.bfloat16):
    result = jax.random.normal(stream_key, extent, jnp.float32) * spread
    if len(cuts) > 0:
        result = block_scale(stream_key, extent, cuts, -0.22, 0.18) * result
    return jnp.clip(result, min=-bound, max=bound).astype(kind)


def setup_inputs(seed: int = 0) -> dict:
    splits = jax.random.split(jax.random.key(seed), 4)
    vectors = bell_draw(splits[0], (STATES, NV), 1.0, 6.0, ((0, 32),), jnp.float32)
    blocks = bell_draw(splits[1], (ROW_BLOCKS, OFFSETS, NBLK, BS, BS), (NBLK * BS * (2 * N_OFF - 1) // TB) ** -0.5, 0.125, ((0, 16), (1, 2)), jnp.float32)
    lists = draw_lists(jax.random.fold_in(splits[3], 71), 0)
    return {"vectors": vectors, "blocks": blocks, "lists": lists}


first_scale = 0.4
later_scale = 0.8


def apply_hamiltonian(field, blocks, lists):
    shaped = field.reshape(ROW_BLOCKS, TB, BS, NV)
    offset_range = jnp.arange(OFFSETS, dtype=jnp.int32)

    def one_row(block_row, totals):
        stored = blocks[block_row]
        row_list = lists[block_row, :, 0, :]
        col_list = lists[block_row, :, 1, :]
        far_rows = ((block_row + offset_range) % ROW_BLOCKS).astype(jnp.int32)
        far_vectors = shaped[far_rows[:, None], col_list]
        own_vectors = shaped[block_row, row_list]
        direct = jnp.einsum("okab,okbv->okav", stored, far_vectors, precision=lax.Precision.HIGHEST)
        transposed = jnp.einsum("okab,okav->okbv", stored, own_vectors, precision=lax.Precision.HIGHEST)
        totals = totals.at[block_row, row_list].add(direct)
        totals = totals.at[far_rows[:, None], col_list].add(transposed)
        return totals

    totals = lax.fori_loop(0, ROW_BLOCKS, one_row, jnp.zeros((ROW_BLOCKS, TB, BS, NV), jnp.float32))
    return totals.reshape(ROW_BLOCKS * TILE, NV)


def reference(vectors, blocks, lists):
    previous = vectors
    current = first_scale * apply_hamiltonian(vectors, blocks, lists)
    for degree in range(1, DEGREE):
        following = later_scale * apply_hamiltonian(current, blocks, lists) - previous
        previous, current = current, following
    return current
```

```python
import functools

import jax
import jax.numpy as jnp
from jax import lax
from jax.experimental import pallas as pl
from jax.experimental.pallas import tpu as pltpu
from jax.sharding import PartitionSpec as P

DEGREE = 4
GROUPS = 2

first_scale = 0.4
later_scale = 0.8

VMEM = pl.BlockSpec(memory_space=pltpu.VMEM)
SMEM = pl.BlockSpec(memory_space=pltpu.SMEM)


def halves(values):
    high = values.astype(jnp.bfloat16)
    low = (values - high.astype(jnp.float32)).astype(jnp.bfloat16)
    return high, low


def product(left, high_ref, low_ref, strip):
    rows, depth = left.shape
    high, low = halves(left)
    both = jnp.concatenate([high, low], axis=0)
    for start in range(0, high_ref.shape[1], strip):
        at = slice(start, start + strip)
        main = jnp.dot(both, high_ref[:, at], preferred_element_type=jnp.float32)
        rest = jnp.dot(high, low_ref[:, at], preferred_element_type=jnp.float32)
        yield at, main[:rows] + main[rows:] + rest


def dense_kernel(lists_ref, blocks_ref, high_ref, low_ref, high_t_ref, low_t_ref):
    size = blocks_ref.shape[-1]
    for ref in (high_ref, low_ref, high_t_ref, low_t_ref):
        ref[...] = jnp.zeros_like(ref)

    @pl.loop(0, blocks_ref.shape[0])
    def _(k):
        row = pl.ds(pl.multiple_of(lists_ref[0, k] * size, size), size)
        col = pl.ds(pl.multiple_of(lists_ref[1, k] * size, size), size)
        block = blocks_ref[k]
        high, low = halves(block)
        high_ref[row, col] = high
        low_ref[row, col] = low
        high, low = halves(block.T)
        high_t_ref[col, row] = high
        low_t_ref[col, row] = low


def first_kernel(n_off, groups, offset_ref, *refs):
    pieces, (high_ref, low_ref), outs = refs[:n_off], refs[n_off : n_off + 2], refs[n_off + 2 :]
    rows = pieces[0].shape[0]
    width = pieces[0].shape[1] // groups
    for step, piece in enumerate(pieces):
        owner = lax.rem(offset_ref[0] - step + n_off, n_off)
        at = pl.ds(pl.multiple_of(owner * rows, rows), rows)
        turned = piece[...].T
        for group in range(groups):
            outs[group][:, at] = turned[group * width : (group + 1) * width]
    for group in range(groups):
        for at, value in product(outs[group][...], high_ref, low_ref, 256):
            outs[groups + group][:, at] = value


def step_kernel(n_off, scale, *refs):
    terms = refs[:n_off]
    has_previous = len(refs) == n_off + 5
    high_ref, low_ref, vectors_ref, out_ref = refs[-4:]
    total = terms[0][...]
    for term in terms[1:]:
        total = total + term[...]
    total = scale * total
    if has_previous:
        total = total - refs[n_off][...]
    vectors_ref[...] = total
    for at, value in product(total, high_ref, low_ref, 256):
        out_ref[:, at] = value


def far_kernel(far_ref, back_ref, high_ref, low_ref, out_ref):
    for at, value in product(far_ref[...], high_ref, low_ref, 256):
        out_ref[:, at] = value + back_ref[:, at]


def last_far_kernel(n_off, offset_ref, far_ref, back_ref, high_ref, low_ref, total_ref, *outs):
    for at, value in product(far_ref[...], high_ref, low_ref, 256):
        total_ref[:, at] = value + back_ref[:, at]
    rows = outs[0].shape[1]
    for step, out in enumerate(outs):
        owner = lax.rem(offset_ref[0] + step, n_off)
        out[...] = total_ref[:, pl.ds(pl.multiple_of(owner * rows, rows), rows)]


def last_kernel(n_off, groups, offset_ref, *refs):
    out_ref = refs[-1]
    rows = out_ref.shape[0]
    at = pl.ds(pl.multiple_of(offset_ref[0] * rows, rows), rows)
    result = []
    for group in range(groups):
        terms = refs[group * n_off : (group + 1) * n_off]
        total = terms[0][...]
        for term in terms[1:]:
            total = total + term[...]
        result.append(later_scale * total - refs[groups * n_off + group][:, at])
    out_ref[...] = jnp.concatenate(result, axis=0).T


def kernel_call(body, in_specs, shapes, scratch=(), flops=0, limit=24):
    return pl.pallas_call(
        body,
        out_shape=shapes,
        in_specs=in_specs,
        out_specs=[VMEM] * len(shapes),
        scratch_shapes=list(scratch),
        compiler_params=pltpu.CompilerParams(vmem_limit_bytes=limit * 2**20),
        cost_estimate=pl.CostEstimate(flops=flops, bytes_accessed=0, transcendentals=0),
    )


def per_device(vectors, blocks, lists):
    n_off = lax.axis_size("off")
    n_row = lax.axis_size("row")
    offset = lax.axis_index("off")[None].astype(jnp.int32)
    piece_rows, width = vectors.shape
    tile_rows = piece_rows * n_off
    group_width = width // GROUPS
    both = ("row", "off")

    def shifted(value, distance):
        return lax.ppermute(value, "off", [(d, (d + distance) % n_off) for d in range(n_off)])

    def route(sign):
        return [
            (i * n_off + d, (i + sign * d) % n_row * n_off + d)
            for i in range(n_row)
            for d in range(n_off)
        ]

    def pull(value):
        return lax.ppermute(value, both, route(-1))

    def push(value):
        return lax.ppermute(value, both, route(1))

    f32 = lambda *shape: jax.ShapeDtypeStruct(shape, jnp.float32)
    bf16 = jax.ShapeDtypeStruct((tile_rows, tile_rows), jnp.bfloat16)
    group_shape = f32(group_width, tile_rows)
    flops = 6 * group_width * tile_rows * tile_rows

    pieces = [vectors] + [shifted(vectors, s) for s in range(1, n_off)]
    high, low, high_t, low_t = kernel_call(
        dense_kernel, [SMEM, VMEM], [bf16] * 4
    )(lists[0, 0], blocks[0, 0])

    outs = kernel_call(
        functools.partial(first_kernel, n_off, GROUPS),
        [SMEM] + [VMEM] * (n_off + 2),
        [group_shape] * (2 * GROUPS),
        flops=flops * GROUPS,
    )(offset, *pieces, high, low)
    current, products = list(outs[:GROUPS]), list(outs[GROUPS:])
    previous = [None] * GROUPS
    totals = [None] * GROUPS
    for degree in range(DEGREE):
        scale = first_scale if degree == 1 else later_scale
        fars, backs = [None] * GROUPS, [None] * GROUPS
        for g in range(GROUPS):
            if degree > 0:
                terms = [totals[g]] + [shifted(totals[g], s) for s in range(1, n_off)]
                older = [] if previous[g] is None else [previous[g]]
                following, products[g] = kernel_call(
                    functools.partial(step_kernel, n_off, scale),
                    [VMEM] * (n_off + len(older) + 2),
                    [group_shape] * 2,
                    flops=flops,
                )(*terms, *older, high, low)
                previous[g], current[g] = current[g], following
            backs[g] = push(products[g])
            fars[g] = pull(current[g])
        for g in range(GROUPS):
            if degree < DEGREE - 1:
                [totals[g]] = kernel_call(
                    far_kernel, [VMEM] * 4, [group_shape], flops=flops
                )(fars[g], backs[g], high_t, low_t)
            else:
                totals[g] = kernel_call(
                    functools.partial(last_far_kernel, n_off),
                    [SMEM] + [VMEM] * 4,
                    [f32(group_width, tile_rows)] + [f32(group_width, piece_rows)] * n_off,
                    flops=flops,
                )(offset, fars[g], backs[g], high_t, low_t)[1:]
    terms = []
    for g in range(GROUPS):
        terms.append(totals[g][0])
        terms.extend(shifted(totals[g][s], s) for s in range(1, n_off))
    [result] = kernel_call(
        functools.partial(last_kernel, n_off, GROUPS),
        [SMEM] + [VMEM] * (GROUPS * (n_off + 1)),
        [f32(piece_rows, width)],
    )(offset, *terms, *previous)
    return result


def solution(mesh):
    in_specs = (
        P(("row", "off"), None),
        P("row", "off", None, None, None),
        P("row", "off", None, None),
    )
    out_specs = P(("row", "off"), None)
    return jax.shard_map(
        per_device, mesh=mesh, in_specs=in_specs, out_specs=out_specs, check_vma=False
    )
```

```python
import functools

import jax
import jax.numpy as jnp
from jax import lax
from jax.experimental import pallas as pl
from jax.experimental.pallas import tpu as pltpu
from jax.sharding import PartitionSpec as P

DEGREE = 4
GROUPS = 2

first_scale = 0.4
later_scale = 0.8

VMEM = pl.BlockSpec(memory_space=pltpu.VMEM)
SMEM = pl.BlockSpec(memory_space=pltpu.SMEM)


def halves(values):
    high = values.astype(jnp.bfloat16)
    low = (values - high.astype(jnp.float32)).astype(jnp.bfloat16)
    return high, low


def product(left, high_ref, low_ref, strip):
    rows, depth = left.shape
    high, low = halves(left)
    both = jnp.concatenate([high, low], axis=0)
    for start in range(0, high_ref.shape[1], strip):
        at = slice(start, start + strip)
        main = jnp.dot(both, high_ref[:, at], preferred_element_type=jnp.float32)
        rest = jnp.dot(high, low_ref[:, at], preferred_element_type=jnp.float32)
        yield at, main[:rows] + main[rows:] + rest


def dense_kernel(turned, which, lists_ref, blocks_ref, high_ref, low_ref):
    size = blocks_ref.shape[-1]
    high_ref[...] = jnp.zeros_like(high_ref)
    low_ref[...] = jnp.zeros_like(low_ref)

    @pl.loop(0, blocks_ref.shape[0])
    def _(k):
        row = pl.ds(pl.multiple_of(lists_ref[which, k] * size, size), size)
        col = pl.ds(pl.multiple_of(lists_ref[1 - which, k] * size, size), size)
        block = blocks_ref[k]
        high_ref[row, col], low_ref[row, col] = halves(block.T if turned else block)


def summed(terms):
    total = terms[0][...]
    for term in terms[1:]:
        total = total + term[...]
    return total


def chosen(refs, at):
    offset = lax.axis_index("off")
    value = refs[0][:, at]
    for distance in range(1, len(refs)):
        value = jnp.where(offset == distance, refs[distance][:, at], value)
    return value


def first_kernel(n_off, groups, *refs):
    pieces, (high_ref, low_ref), outs = refs[:n_off], refs[n_off : n_off + 2], refs[n_off + 2 :]
    rows = pieces[0].shape[0]
    width = pieces[0].shape[1] // groups
    offset = lax.axis_index("off")
    for step, piece in enumerate(pieces):
        owner = lax.rem(offset - step + n_off, n_off)
        at = pl.ds(pl.multiple_of(owner * rows, rows), rows)
        turned = piece[...].T
        for group in range(groups):
            outs[group][:, at] = turned[group * width : (group + 1) * width]
    for group in range(groups):
        for at, value in product(outs[group][...], high_ref, low_ref, 256):
            outs[groups + group][:, at] = value


def step_kernel(n_off, scale, *refs):
    high_ref, low_ref, vectors_ref, out_ref = refs[-4:]
    total = scale * summed(refs[:n_off])
    if len(refs) > n_off + 4:
        total = total - refs[n_off][...]
    vectors_ref[...] = total
    for at, value in product(total, high_ref, low_ref, 256):
        out_ref[:, at] = value


def far_kernel(n_off, *refs):
    fars, backs = refs[:n_off], refs[n_off : 2 * n_off]
    high_ref, low_ref = refs[2 * n_off : 2 * n_off + 2]
    total_ref, outs = refs[2 * n_off + 2], refs[2 * n_off + 3 :]
    everything = slice(None)
    for at, value in product(chosen(fars, everything), high_ref, low_ref, 256):
        total_ref[:, at] = value + chosen(backs, at)
    for step, out in enumerate(outs):
        rows = out.shape[1]
        owner = lax.rem(lax.axis_index("off") + step, n_off)
        out[...] = total_ref[:, pl.ds(pl.multiple_of(owner * rows, rows), rows)]


def last_kernel(n_off, groups, *refs):
    out_ref = refs[-1]
    rows = out_ref.shape[0]
    at = pl.ds(pl.multiple_of(lax.axis_index("off") * rows, rows), rows)
    result = []
    for group in range(groups):
        total = summed(refs[group * n_off : (group + 1) * n_off])
        result.append(later_scale * total - refs[groups * n_off + group][:, at])
    out_ref[...] = jnp.concatenate(result, axis=0).T


def kernel_call(body, in_specs, shapes, scratch=(), flops=0, limit=24):
    return pl.pallas_call(
        body,
        out_shape=shapes,
        in_specs=in_specs,
        out_specs=[VMEM] * len(shapes),
        scratch_shapes=list(scratch),
        compiler_params=pltpu.CompilerParams(vmem_limit_bytes=limit * 2**20),
        cost_estimate=pl.CostEstimate(flops=flops, bytes_accessed=0, transcendentals=0),
    )


def per_device(vectors, blocks, lists):
    n_off = lax.axis_size("off")
    n_row = lax.axis_size("row")
    piece_rows, width = vectors.shape
    tile_rows = piece_rows * n_off
    group_width = width // GROUPS

    def shifted(value, distance):
        return lax.ppermute(value, "off", [(d, (d + distance) % n_off) for d in range(n_off)])

    def passed(value, direction):
        route = [(i, (i + direction) % n_row) for i in range(n_row)]
        values = [value]
        for _ in range(1, n_off):
            values.append(lax.ppermute(values[-1], "row", route))
        return values

    f32 = lambda *shape: jax.ShapeDtypeStruct(shape, jnp.float32)
    bf16 = jax.ShapeDtypeStruct((tile_rows, tile_rows), jnp.bfloat16)
    group_shape = f32(group_width, tile_rows)
    piece_shape = f32(group_width, piece_rows)
    flops = 6 * group_width * tile_rows * tile_rows

    pieces = [vectors] + [shifted(vectors, s) for s in range(1, n_off)]
    high, low = kernel_call(
        functools.partial(dense_kernel, False, 0), [SMEM, VMEM], [bf16] * 2
    )(lists[0, 0], blocks[0, 0])
    outs = kernel_call(
        functools.partial(first_kernel, n_off, GROUPS),
        [VMEM] * (n_off + 2),
        [group_shape] * (2 * GROUPS),
        flops=flops * GROUPS,
    )(*pieces, high, low)
    high_t, low_t = kernel_call(
        functools.partial(dense_kernel, True, 1), [SMEM, VMEM], [bf16] * 2, flops=flops
    )(lists[0, 0], blocks[0, 0])

    current, products = list(outs[:GROUPS]), list(outs[GROUPS:])
    previous = [None] * GROUPS
    totals = [None] * GROUPS
    for degree in range(DEGREE):
        scale = first_scale if degree == 1 else later_scale
        fars, backs = [None] * GROUPS, [None] * GROUPS
        for g in range(GROUPS):
            if degree > 0:
                terms = [totals[g]] + [shifted(totals[g], s) for s in range(1, n_off)]
                older = [] if previous[g] is None else [previous[g]]
                following, products[g] = kernel_call(
                    functools.partial(step_kernel, n_off, scale),
                    [VMEM] * (n_off + len(older) + 2),
                    [group_shape] * 2,
                    flops=flops,
                )(*terms, *older, high, low)
                previous[g], current[g] = current[g], following
            backs[g] = passed(products[g], 1)
            fars[g] = passed(current[g], -1)
        for g in range(GROUPS):
            pieces_out = n_off if degree == DEGREE - 1 else 0
            outs = kernel_call(
                functools.partial(far_kernel, n_off),
                [VMEM] * (2 * n_off + 2),
                [group_shape] + [piece_shape] * pieces_out,
                flops=flops,
            )(*fars[g], *backs[g], high_t, low_t)
            totals[g] = outs[1:] if pieces_out else outs[0]
    terms = []
    for g in range(GROUPS):
        terms.append(totals[g][0])
        terms.extend(shifted(totals[g][s], s) for s in range(1, n_off))
    [result] = kernel_call(
        functools.partial(last_kernel, n_off, GROUPS),
        [VMEM] * (GROUPS * (n_off + 1)),
        [f32(piece_rows, width)],
    )(*terms, *previous)
    return result


def solution(mesh):
    in_specs = (
        P(("row", "off"), None),
        P("row", "off", None, None, None),
        P("row", "off", None, None),
    )
    out_specs = P(("row", "off"), None)
    return jax.shard_map(
        per_device, mesh=mesh, in_specs=in_specs, out_specs=out_specs, check_vma=False
    )
```

```python
import functools
import math

import jax
import jax.numpy as jnp
from jax import lax
from jax.experimental import pallas as pl
from jax.experimental.pallas import tpu as pltpu
from jax.sharding import PartitionSpec as P

DEGREE = 4
GROUPS = 2
UNROLL = 4

first_scale = 0.4
later_scale = 0.8

VMEM = pl.BlockSpec(memory_space=pltpu.VMEM)
SMEM = pl.BlockSpec(memory_space=pltpu.SMEM)


def halves(values):
    high = values.astype(jnp.bfloat16)
    low = (values - high.astype(jnp.float32)).astype(jnp.bfloat16)
    return high, low


def product(left, high_ref, low_ref, strip):
    rows, depth = left.shape
    high, low = halves(left)
    both = jnp.concatenate([high, low], axis=0)
    for start in range(0, high_ref.shape[1], strip):
        at = slice(start, start + strip)
        main = jnp.dot(both, high_ref[:, at], preferred_element_type=jnp.float32)
        rest = jnp.dot(high, low_ref[:, at], preferred_element_type=jnp.float32)
        yield at, main[:rows] + main[rows:] + rest


def dense_kernel(lists_ref, blocks_ref, high_ref, low_ref, high_t_ref, low_t_ref):
    size = blocks_ref.shape[-1]
    for ref in (high_ref, low_ref, high_t_ref, low_t_ref):
        ref[...] = jnp.zeros_like(ref)

    @pl.loop(0, blocks_ref.shape[0], unroll=UNROLL)
    def _(k):
        row = pl.ds(pl.multiple_of(lists_ref[0, k] * size, size), size)
        col = pl.ds(pl.multiple_of(lists_ref[1, k] * size, size), size)
        block = blocks_ref[k]
        high_ref[row, col], low_ref[row, col] = halves(block)
        high_t_ref[col, row], low_t_ref[col, row] = halves(block.T)


def summed(terms):
    total = terms[0][...]
    for term in terms[1:]:
        total = total + term[...]
    return total


def partner_order(n_off, n_row):
    offset, row = lax.axis_index("off"), lax.axis_index("row")
    ahead_first = offset >= 0
    for distance in range(1, n_off):
        parity = lax.rem(lax.div(row, math.gcd(distance, n_row)), 2)
        ahead_first = jnp.where(offset == distance, parity == 0, ahead_first)
    return ahead_first


def write_products(ahead_first, total, high_ref, low_ref, first_ref, second_ref):
    for at, value in product(total, high_ref, low_ref, 256):
        first_ref[:, at] = jnp.where(ahead_first, value, total[:, at])
        second_ref[:, at] = jnp.where(ahead_first, total[:, at], value)


def turn_kernel(groups, piece_ref, *outs):
    turned = piece_ref[...].T
    width = turned.shape[0] // groups
    for group, out in enumerate(outs):
        out[...] = turned[group * width : (group + 1) * width]


def first_kernel(n_off, n_row, *refs):
    pieces, (high_ref, low_ref, vectors_ref, first_ref, second_ref) = refs[:n_off], refs[n_off:]
    rows = pieces[0].shape[1]
    for step, piece in enumerate(pieces):
        owner = lax.rem(lax.axis_index("off") - step + n_off, n_off)
        vectors_ref[:, pl.ds(pl.multiple_of(owner * rows, rows), rows)] = piece[...]
    write_products(
        partner_order(n_off, n_row), vectors_ref[...], high_ref, low_ref, first_ref, second_ref
    )


def step_kernel(n_off, n_row, scale, *refs):
    high_ref, low_ref, vectors_ref, first_ref, second_ref = refs[-5:]
    total = scale * summed(refs[:n_off])
    if len(refs) > n_off + 5:
        total = total - refs[n_off][...]
    vectors_ref[...] = total
    write_products(partner_order(n_off, n_row), total, high_ref, low_ref, first_ref, second_ref)


def far_kernel(n_off, n_row, *refs):
    seconds, firsts = refs[:n_off], refs[n_off : 2 * n_off]
    high_ref, low_ref, total_ref, *outs = refs[2 * n_off :]
    offset = lax.axis_index("off")
    ahead_first = partner_order(n_off, n_row)

    def chosen(own, if_ahead, if_not, at):
        value = own[:, at]
        for distance in range(1, n_off):
            swapped = jnp.where(ahead_first, if_ahead[distance][:, at], if_not[distance][:, at])
            value = jnp.where(offset == distance, swapped, value)
        return value

    far = chosen(seconds[0], firsts, seconds, slice(None))
    for at, value in product(far, high_ref, low_ref, 256):
        total_ref[:, at] = value + chosen(firsts[0], seconds, firsts, at)
    for step, out in enumerate(outs):
        rows = out.shape[1]
        owner = lax.rem(offset + step, n_off)
        out[...] = total_ref[:, pl.ds(pl.multiple_of(owner * rows, rows), rows)]


def last_kernel(n_off, groups, *refs):
    out_ref = refs[-1]
    rows = out_ref.shape[0]
    at = pl.ds(pl.multiple_of(lax.axis_index("off") * rows, rows), rows)
    result = []
    for group in range(groups):
        total = summed(refs[group * n_off : (group + 1) * n_off])
        result.append(later_scale * total - refs[groups * n_off + group][:, at])
    out_ref[...] = jnp.concatenate(result, axis=0).T


def kernel_call(body, in_specs, shapes, scratch=(), flops=0, limit=24):
    return pl.pallas_call(
        body,
        out_shape=shapes,
        in_specs=in_specs,
        out_specs=[VMEM] * len(shapes),
        scratch_shapes=list(scratch),
        compiler_params=pltpu.CompilerParams(vmem_limit_bytes=limit * 2**20),
        cost_estimate=pl.CostEstimate(flops=flops, bytes_accessed=0, transcendentals=0),
    )


def per_device(vectors, blocks, lists):
    n_off = lax.axis_size("off")
    n_row = lax.axis_size("row")
    piece_rows, width = vectors.shape
    tile_rows = piece_rows * n_off
    group_width = width // GROUPS

    def shifted(value, distance):
        return lax.ppermute(value, "off", [(d, (d + distance) % n_off) for d in range(n_off)])

    def swapped(value, ahead):
        values = [value]
        for distance in range(1, n_off):
            step = math.gcd(distance, n_row)
            assert n_row // step % 2 == 0
            route = [
                (i, (i + (distance if (i // step + ahead) % 2 else -distance)) % n_row)
                for i in range(n_row)
            ]
            values.append(lax.ppermute(value, "row", route))
        return values

    f32 = lambda *shape: jax.ShapeDtypeStruct(shape, jnp.float32)
    bf16 = jax.ShapeDtypeStruct((tile_rows, tile_rows), jnp.bfloat16)
    group_shape = f32(group_width, tile_rows)
    piece_shape = f32(group_width, piece_rows)
    flops = 6 * group_width * tile_rows * tile_rows

    pieces = kernel_call(functools.partial(turn_kernel, GROUPS), [VMEM], [piece_shape] * GROUPS)(
        vectors
    )
    pieces = [[piece] + [shifted(piece, s) for s in range(1, n_off)] for piece in pieces]
    high, low, high_t, low_t = kernel_call(
        dense_kernel, [SMEM, VMEM], [bf16] * 4, flops=flops
    )(lists[0, 0], blocks[0, 0])

    older, newer = [None] * GROUPS, [None] * GROUPS
    totals = [None] * GROUPS
    for degree in range(DEGREE):
        scale = first_scale if degree == 1 else later_scale
        firsts, seconds = [None] * GROUPS, [None] * GROUPS
        for g in range(GROUPS):
            if degree == 0:
                body = functools.partial(first_kernel, n_off, n_row)
                terms = pieces[g]
            else:
                body = functools.partial(step_kernel, n_off, n_row, scale)
                terms = [totals[g]] + [shifted(totals[g], s) for s in range(1, n_off)]
                terms += [older[g]] if degree > 1 else []
            older[g] = newer[g]
            newer[g], first, second = kernel_call(
                body, [VMEM] * (len(terms) + 2), [group_shape] * 3, flops=flops
            )(*terms, high, low)
            seconds[g] = swapped(second, 0)
            firsts[g] = swapped(first, 1)
        for g in range(GROUPS):
            pieces_out = n_off if degree == DEGREE - 1 else 0
            outs = kernel_call(
                functools.partial(far_kernel, n_off, n_row),
                [VMEM] * (2 * n_off + 2),
                [group_shape] + [piece_shape] * pieces_out,
                flops=flops,
            )(*seconds[g], *firsts[g], high_t, low_t)
            totals[g] = outs[1:] if pieces_out else outs[0]
    terms = []
    for g in range(GROUPS):
        terms.append(totals[g][0])
        terms.extend(shifted(totals[g][s], s) for s in range(1, n_off))
    [result] = kernel_call(
        functools.partial(last_kernel, n_off, GROUPS),
        [VMEM] * (GROUPS * (n_off + 1)),
        [f32(piece_rows, width)],
    )(*terms, *older)
    return result


def solution(mesh):
    in_specs = (
        P(("row", "off"), None),
        P("row", "off", None, None, None),
        P("row", "off", None, None),
    )
    out_specs = P(("row", "off"), None)
    return jax.shard_map(
        per_device, mesh=mesh, in_specs=in_specs, out_specs=out_specs, check_vma=False
    )
```

```python
import functools
import math

import jax
import jax.numpy as jnp
from jax import lax
from jax.experimental import pallas as pl
from jax.experimental.pallas import tpu as pltpu
from jax.sharding import PartitionSpec as P

DEGREE = 4
GROUPS = 2
UNROLL = 4
CHUNKS = 4

first_scale = 0.4
later_scale = 0.8

VMEM = pl.BlockSpec(memory_space=pltpu.VMEM)
HBM = pl.BlockSpec(memory_space=pltpu.HBM)


def halves(values):
    high = values.astype(jnp.bfloat16)
    low = (values - high.astype(jnp.float32)).astype(jnp.bfloat16)
    return high, low


def product(left, high_ref, low_ref, strip):
    rows, depth = left.shape
    high, low = halves(left)
    both = jnp.concatenate([high, low], axis=0)
    for start in range(0, high_ref.shape[1], strip):
        at = slice(start, start + strip)
        main = jnp.dot(both, high_ref[:, at], preferred_element_type=jnp.float32)
        rest = jnp.dot(high, low_ref[:, at], preferred_element_type=jnp.float32)
        yield at, main[:rows] + main[rows:] + rest


def dense_kernel(lists_hbm, blocks_hbm, high_ref, low_ref, lists_ref, blocks_ref, semaphores):
    count, size = blocks_ref.shape[0], blocks_ref.shape[-1]
    chunk = count // math.gcd(count, CHUNKS)
    copies = [pltpu.make_async_copy(lists_hbm.at[0, 0], lists_ref, semaphores.at[0])]
    for at, start in enumerate(range(0, count, chunk)):
        part = pl.ds(start, chunk)
        copies.append(
            pltpu.make_async_copy(
                blocks_hbm.at[0, 0, part], blocks_ref.at[part], semaphores.at[1 + at]
            )
        )
    for copy in copies:
        copy.start()
    high_ref[...] = jnp.zeros_like(high_ref)
    low_ref[...] = jnp.zeros_like(low_ref)
    copies[0].wait()
    for at, copy in enumerate(copies[1:]):
        copy.wait()

        @pl.loop(at * chunk, (at + 1) * chunk, unroll=UNROLL)
        def _(k):
            row = pl.ds(pl.multiple_of(lists_ref[0, k] * size, size), size)
            col = pl.ds(pl.multiple_of(lists_ref[1, k] * size, size), size)
            high_ref[row, col], low_ref[row, col] = halves(blocks_ref[k])


def transpose_kernel(high_ref, low_ref, high_t_ref, low_t_ref):
    for start in range(0, high_ref.shape[0], 128):
        at = slice(start, start + 128)
        high_t_ref[at, :] = high_ref[:, at].T
        low_t_ref[at, :] = low_ref[:, at].T


def summed(terms):
    total = terms[0][...]
    for term in terms[1:]:
        total = total + term[...]
    return total


def partner_order(n_off, n_row):
    offset, row = lax.axis_index("off"), lax.axis_index("row")
    ahead_first = offset >= 0
    for distance in range(1, n_off):
        parity = lax.rem(lax.div(row, math.gcd(distance, n_row)), 2)
        ahead_first = jnp.where(offset == distance, parity == 0, ahead_first)
    return ahead_first


def write_products(ahead_first, total, high_ref, low_ref, first_ref, second_ref):
    for at, value in product(total, high_ref, low_ref, 256):
        second_ref[:, at] = jnp.where(ahead_first, total[:, at], value)
        first_ref[:, at] = jnp.where(ahead_first, value, total[:, at])


def turn_kernel(groups, piece_ref, *outs):
    turned = piece_ref[...].T
    width = turned.shape[0] // groups
    for group, out in enumerate(outs):
        out[...] = turned[group * width : (group + 1) * width]


def first_kernel(n_off, n_row, *refs):
    pieces, (high_ref, low_ref) = refs[:n_off], refs[n_off : n_off + 2]
    vectors_ref, second_ref, first_ref = refs[-3:]
    rows = pieces[0].shape[1]
    for step, piece in enumerate(pieces):
        owner = lax.rem(lax.axis_index("off") - step + n_off, n_off)
        vectors_ref[:, pl.ds(pl.multiple_of(owner * rows, rows), rows)] = piece[...]
    write_products(
        partner_order(n_off, n_row),
        vectors_ref[...],
        high_ref,
        low_ref,
        first_ref,
        second_ref,
    )


def step_kernel(n_off, n_row, scale, has_older, keeps, *refs):
    total = scale * summed(refs[:n_off])
    if has_older:
        total = total - refs[n_off][...]
    if keeps:
        refs[-3][...] = total
    high_ref, low_ref = refs[n_off + has_older : n_off + has_older + 2]
    second_ref, first_ref = refs[-2:]
    write_products(
        partner_order(n_off, n_row), total, high_ref, low_ref, first_ref, second_ref
    )


def far_kernel(n_off, n_row, *refs):
    seconds, firsts = refs[:n_off], refs[n_off : 2 * n_off]
    high_ref, low_ref, *outs = refs[2 * n_off :]
    offset = lax.axis_index("off")
    ahead_first = partner_order(n_off, n_row)

    def far(at):
        value = seconds[0][:, at]
        for distance in range(1, n_off):
            swapped = jnp.where(ahead_first, firsts[distance][:, at], seconds[distance][:, at])
            value = jnp.where(offset == distance, swapped, value)
        return value

    def back(at):
        value = firsts[0][:, at]
        for distance in range(1, n_off):
            swapped = jnp.where(ahead_first, seconds[distance][:, at], firsts[distance][:, at])
            value = jnp.where(offset == distance, swapped, value)
        return value

    total_ref = outs[-1]
    for at, value in product(far(slice(None)), high_ref, low_ref, 256):
        total_ref[:, at] = value + back(at)
    for step, out in enumerate(outs[:-1]):
        rows_out = out.shape[1]
        owner = lax.rem(offset + step, n_off)
        out[...] = total_ref[:, pl.ds(pl.multiple_of(owner * rows_out, rows_out), rows_out)]


def last_kernel(n_off, groups, *refs):
    out_ref = refs[-1]
    rows = out_ref.shape[0]
    at = pl.ds(pl.multiple_of(lax.axis_index("off") * rows, rows), rows)
    result = []
    for group in range(groups):
        total = summed(refs[group * n_off : (group + 1) * n_off])
        result.append(later_scale * total - refs[groups * n_off + group][:, at])
    out_ref[...] = jnp.concatenate(result, axis=0).T


def kernel_call(body, in_specs, shapes, scratch=(), flops=0):
    return pl.pallas_call(
        body,
        out_shape=shapes,
        in_specs=in_specs,
        out_specs=[VMEM] * len(shapes),
        scratch_shapes=list(scratch),
        compiler_params=pltpu.CompilerParams(vmem_limit_bytes=24 * 2**20),
        cost_estimate=pl.CostEstimate(flops=flops, bytes_accessed=0, transcendentals=0),
    )


def per_device(vectors, blocks, lists):
    n_off = lax.axis_size("off")
    n_row = lax.axis_size("row")
    piece_rows, width = vectors.shape
    tile_rows = piece_rows * n_off
    group_width = width // GROUPS

    def shifted(value, distance):
        return lax.ppermute(value, "off", [(d, (d + distance) % n_off) for d in range(n_off)])

    def swapped(value, ahead):
        values = [value]
        for distance in range(1, n_off):
            step = math.gcd(distance, n_row)
            assert n_row // step % 2 == 0
            route = [
                (i, (i + (distance if (i // step + ahead) % 2 else -distance)) % n_row)
                for i in range(n_row)
            ]
            values.append(lax.ppermute(value, "row", route))
        return values

    f32 = lambda *shape: jax.ShapeDtypeStruct(shape, jnp.float32)
    bf16 = jax.ShapeDtypeStruct((tile_rows, tile_rows), jnp.bfloat16)
    group_shape = f32(group_width, tile_rows)
    piece_shape = f32(group_width, piece_rows)
    flops = 6 * group_width * tile_rows * tile_rows

    pieces = kernel_call(functools.partial(turn_kernel, GROUPS), [VMEM], [piece_shape] * GROUPS)(
        vectors
    )
    pieces = [[piece] + [shifted(piece, s) for s in range(1, n_off)] for piece in pieces]
    count = blocks.shape[2]
    high, low = kernel_call(
        dense_kernel,
        [HBM, HBM],
        [bf16] * 2,
        [
            pltpu.SMEM(lists.shape[2:], lists.dtype),
            pltpu.VMEM(blocks.shape[2:], blocks.dtype),
            pltpu.SemaphoreType.DMA((1 + math.gcd(count, CHUNKS),)),
        ],
    )(*(pltpu.with_memory_space_constraint(x, pltpu.HBM) for x in (lists, blocks)))
    high_t, low_t = kernel_call(transpose_kernel, [VMEM] * 2, [bf16] * 2, flops=flops)(high, low)

    older, newer = [None] * GROUPS, [None] * GROUPS
    totals = [None] * GROUPS
    for degree in range(DEGREE):
        scale = first_scale if degree == 1 else later_scale
        last = degree == DEGREE - 1
        seconds = []
        firsts = []
        for g in range(GROUPS):
            if degree == 0:
                body = functools.partial(first_kernel, n_off, n_row)
                terms = pieces[g]
            else:
                body = functools.partial(
                    step_kernel, n_off, n_row, scale, int(degree > 1), not last
                )
                terms = [totals[g]] + [shifted(totals[g], s) for s in range(1, n_off)]
                terms += [older[g]] if degree > 1 else []
            kept = [] if last else [group_shape]
            *kept, second, first = kernel_call(
                body, [VMEM] * (len(terms) + 2), kept + [group_shape] * 2, flops=flops
            )(*terms, high, low)
            older[g], newer[g] = newer[g], kept[0] if kept else None
            seconds.append(swapped(second, 0))
            firsts.append(swapped(first, 1))
        for g in range(GROUPS):
            outs = kernel_call(
                functools.partial(far_kernel, n_off, n_row),
                [VMEM] * (2 * n_off + 2),
                [piece_shape] * n_off if last else [group_shape],
                [pltpu.VMEM(group_shape.shape, jnp.float32)] if last else [],
                flops=flops,
            )(*seconds[g], *firsts[g], high_t, low_t)
            totals[g] = outs if last else outs[0]
    terms = []
    for g in range(GROUPS):
        terms.append(totals[g][0])
        terms.extend(shifted(totals[g][s], s) for s in range(1, n_off))
    [result] = kernel_call(
        functools.partial(last_kernel, n_off, GROUPS),
        [VMEM] * (GROUPS * (n_off + 1)),
        [f32(piece_rows, width)],
    )(*terms, *older)
    return result


def solution(mesh):
    in_specs = (
        P(("row", "off"), None),
        P("row", "off", None, None, None),
        P("row", "off", None, None),
    )
    out_specs = P(("row", "off"), None)
    return jax.shard_map(
        per_device, mesh=mesh, in_specs=in_specs, out_specs=out_specs, check_vma=False
    )
```

```python
import functools
import math

import jax
import jax.numpy as jnp
from jax import lax
from jax.experimental import pallas as pl
from jax.experimental.pallas import tpu as pltpu
from jax.sharding import PartitionSpec as P

DEGREE = 4
GROUPS = 2
UNROLL = 4
CHUNKS = 4

first_scale = 0.4
later_scale = 0.8

VMEM = pl.BlockSpec(memory_space=pltpu.VMEM)
HBM = pl.BlockSpec(memory_space=pltpu.HBM)


def halves(values):
    high = values.astype(jnp.bfloat16)
    low = (values - high.astype(jnp.float32)).astype(jnp.bfloat16)
    return high, low


def product(left, high_ref, low_ref, strip):
    rows, depth = left.shape
    high, low = halves(left)
    both = jnp.concatenate([high, low], axis=0)
    for start in range(0, high_ref.shape[1], strip):
        at = slice(start, start + strip)
        main = jnp.dot(both, high_ref[:, at], preferred_element_type=jnp.float32)
        rest = jnp.dot(high, low_ref[:, at], preferred_element_type=jnp.float32)
        yield at, main[:rows] + main[rows:] + rest


def dense_kernel(lists_hbm, blocks_hbm, high_ref, low_ref, lists_ref, blocks_ref, semaphores):
    count, size = blocks_ref.shape[0], blocks_ref.shape[-1]
    chunk = count // math.gcd(count, CHUNKS)
    copies = [pltpu.make_async_copy(lists_hbm.at[0, 0], lists_ref, semaphores.at[0])]
    for at, start in enumerate(range(0, count, chunk)):
        part = pl.ds(start, chunk)
        copies.append(
            pltpu.make_async_copy(
                blocks_hbm.at[0, 0, part], blocks_ref.at[part], semaphores.at[1 + at]
            )
        )
    for copy in copies:
        copy.start()
    high_ref[...] = jnp.zeros_like(high_ref)
    low_ref[...] = jnp.zeros_like(low_ref)
    copies[0].wait()
    for at, copy in enumerate(copies[1:]):
        copy.wait()

        @pl.loop(at * chunk, (at + 1) * chunk, unroll=UNROLL)
        def _(k):
            row = pl.ds(pl.multiple_of(lists_ref[0, k] * size, size), size)
            col = pl.ds(pl.multiple_of(lists_ref[1, k] * size, size), size)
            high_ref[row, col], low_ref[row, col] = halves(blocks_ref[k])


def transpose_kernel(high_ref, low_ref, high_t_ref, low_t_ref):
    for start in range(0, high_ref.shape[0], 128):
        at = slice(start, start + 128)
        high_t_ref[at, :] = high_ref[:, at].T
        low_t_ref[at, :] = low_ref[:, at].T


def summed(terms):
    total = terms[0][...]
    for term in terms[1:]:
        total = total + term[...]
    return total


def partner_order(n_off, n_row):
    offset, row = lax.axis_index("off"), lax.axis_index("row")
    ahead_first = offset >= 0
    for distance in range(1, n_off):
        parity = lax.rem(lax.div(row, math.gcd(distance, n_row)), 2)
        ahead_first = jnp.where(offset == distance, parity == 0, ahead_first)
    return ahead_first


def write_products(ahead_first, total, high_ref, low_ref, first_ref, second_ref):
    for at, value in product(total, high_ref, low_ref, 256):
        second_ref[:, at] = jnp.where(ahead_first, total[:, at], value)
        first_ref[:, at] = jnp.where(ahead_first, value, total[:, at])


def turn_kernel(groups, piece_ref, *outs):
    turned = piece_ref[...].T
    width = turned.shape[0] // groups
    for group, out in enumerate(outs):
        out[...] = turned[group * width : (group + 1) * width]


def first_kernel(n_off, n_row, *refs):
    pieces, (high_ref, low_ref) = refs[:n_off], refs[n_off : n_off + 2]
    vectors_ref, second_ref, first_ref = refs[-3:]
    rows = pieces[0].shape[1]
    for step, piece in enumerate(pieces):
        owner = lax.rem(lax.axis_index("off") - step + n_off, n_off)
        vectors_ref[:, pl.ds(pl.multiple_of(owner * rows, rows), rows)] = piece[...]
    write_products(
        partner_order(n_off, n_row),
        vectors_ref[...],
        high_ref,
        low_ref,
        first_ref,
        second_ref,
    )


def step_kernel(n_off, n_row, scale, has_older, keeps, *refs):
    total = scale * summed(refs[:n_off])
    if has_older:
        total = total - refs[n_off][...]
    if keeps:
        refs[-3][...] = total
    high_ref, low_ref = refs[n_off + has_older : n_off + has_older + 2]
    second_ref, first_ref = refs[-2:]
    write_products(
        partner_order(n_off, n_row), total, high_ref, low_ref, first_ref, second_ref
    )


def far_kernel(n_off, n_row, *refs):
    own_second, second, own_first, first, high_ref, low_ref, *outs = refs
    offset = lax.axis_index("off")
    ahead_first = partner_order(n_off, n_row)

    def received(own, if_ahead, if_not, at):
        value = jnp.where(ahead_first, if_ahead[:, at], if_not[:, at])
        return jnp.where(offset == 0, own[:, at], value)

    total_ref = outs[-1]
    far = received(own_second, first, second, slice(None))
    for at, value in product(far, high_ref, low_ref, 256):
        total_ref[:, at] = value + received(own_first, second, first, at)
    for step, out in enumerate(outs[:-1]):
        rows = out.shape[1]
        owner = lax.rem(offset + step, n_off)
        out[...] = total_ref[:, pl.ds(pl.multiple_of(owner * rows, rows), rows)]


def last_kernel(n_off, groups, *refs):
    out_ref = refs[-1]
    rows = out_ref.shape[0]
    at = pl.ds(pl.multiple_of(lax.axis_index("off") * rows, rows), rows)
    result = []
    for group in range(groups):
        total = summed(refs[group * n_off : (group + 1) * n_off])
        result.append(later_scale * total - refs[groups * n_off + group][:, at])
    out_ref[...] = jnp.concatenate(result, axis=0).T


def kernel_call(body, in_specs, shapes, scratch=(), flops=0):
    return pl.pallas_call(
        body,
        out_shape=shapes,
        in_specs=in_specs,
        out_specs=[VMEM] * len(shapes),
        scratch_shapes=list(scratch),
        compiler_params=pltpu.CompilerParams(vmem_limit_bytes=24 * 2**20),
        cost_estimate=pl.CostEstimate(flops=flops, bytes_accessed=0, transcendentals=0),
    )


def per_device(vectors, blocks, lists):
    n_off = lax.axis_size("off")
    n_row = lax.axis_size("row")
    piece_rows, width = vectors.shape
    tile_rows = piece_rows * n_off
    group_width = width // GROUPS

    def shifted(value, distance):
        return lax.ppermute(value, "off", [(d, (d + distance) % n_off) for d in range(n_off)])

    def swapped(value, ahead):
        route = []
        for i in range(n_row):
            for d in range(n_off):
                step = math.gcd(d, n_row) if d else 1
                assert n_row // step % 2 == 0
                forward = i // step % 2 == (1 - ahead if d else 0)
                partner = (i + (d or 1) * (1 if forward else -1)) % n_row
                route.append((i * n_off + d, partner * n_off + d))
        return [value, lax.ppermute(value, ("row", "off"), route)]

    f32 = lambda *shape: jax.ShapeDtypeStruct(shape, jnp.float32)
    bf16 = jax.ShapeDtypeStruct((tile_rows, tile_rows), jnp.bfloat16)
    group_shape = f32(group_width, tile_rows)
    piece_shape = f32(group_width, piece_rows)
    flops = 6 * group_width * tile_rows * tile_rows

    pieces = kernel_call(functools.partial(turn_kernel, GROUPS), [VMEM], [piece_shape] * GROUPS)(
        vectors
    )
    pieces = [[piece] + [shifted(piece, s) for s in range(1, n_off)] for piece in pieces]
    count = blocks.shape[2]
    high, low = kernel_call(
        dense_kernel,
        [HBM, HBM],
        [bf16] * 2,
        [
            pltpu.SMEM(lists.shape[2:], lists.dtype),
            pltpu.VMEM(blocks.shape[2:], blocks.dtype),
            pltpu.SemaphoreType.DMA((1 + math.gcd(count, CHUNKS),)),
        ],
    )(*(pltpu.with_memory_space_constraint(x, pltpu.HBM) for x in (lists, blocks)))
    high_t, low_t = kernel_call(transpose_kernel, [VMEM] * 2, [bf16] * 2, flops=flops)(high, low)

    older, newer = [None] * GROUPS, [None] * GROUPS
    totals = [None] * GROUPS
    for degree in range(DEGREE):
        scale = first_scale if degree == 1 else later_scale
        last = degree == DEGREE - 1
        seconds = []
        firsts = []
        for g in range(GROUPS):
            if degree == 0:
                body = functools.partial(first_kernel, n_off, n_row)
                terms = pieces[g]
            else:
                body = functools.partial(
                    step_kernel, n_off, n_row, scale, int(degree > 1), not last
                )
                terms = [totals[g]] + [shifted(totals[g], s) for s in range(1, n_off)]
                terms += [older[g]] if degree > 1 else []
            kept = [] if last else [group_shape]
            *kept, second, first = kernel_call(
                body, [VMEM] * (len(terms) + 2), kept + [group_shape] * 2, flops=flops
            )(*terms, high, low)
            older[g], newer[g] = newer[g], kept[0] if kept else None
            seconds.append(swapped(second, 0))
            firsts.append(swapped(first, 1))
        for g in range(GROUPS):
            outs = kernel_call(
                functools.partial(far_kernel, n_off, n_row),
                [VMEM] * 6,
                [piece_shape] * n_off if last else [group_shape],
                [pltpu.VMEM(group_shape.shape, jnp.float32)] if last else [],
                flops=flops,
            )(*seconds[g], *firsts[g], high_t, low_t)
            totals[g] = outs if last else outs[0]
    terms = []
    for g in range(GROUPS):
        terms.append(totals[g][0])
        terms.extend(shifted(totals[g][s], s) for s in range(1, n_off))
    [result] = kernel_call(
        functools.partial(last_kernel, n_off, GROUPS),
        [VMEM] * (GROUPS * (n_off + 1)),
        [f32(piece_rows, width)],
    )(*terms, *older)
    return result


def solution(mesh):
    in_specs = (
        P(("row", "off"), None),
        P("row", "off", None, None, None),
        P("row", "off", None, None),
    )
    out_specs = P(("row", "off"), None)
    return jax.shard_map(
        per_device, mesh=mesh, in_specs=in_specs, out_specs=out_specs, check_vma=False
    )
```

```python
import functools
import math

import jax
import jax.numpy as jnp
from jax import lax
from jax.experimental import pallas as pl
from jax.experimental.pallas import tpu as pltpu
from jax.sharding import PartitionSpec as P

DEGREE = 4
GROUPS = 2
UNROLL = 4
CHUNKS = 4

first_scale = 0.4
later_scale = 0.8

VMEM = pl.BlockSpec(memory_space=pltpu.VMEM)
HBM = pl.BlockSpec(memory_space=pltpu.HBM)


def halves(values):
    high = values.astype(jnp.bfloat16)
    low = (values - high.astype(jnp.float32)).astype(jnp.bfloat16)
    return high, low


def product(left, high_ref, low_ref, strip):
    rows, depth = left.shape
    high, low = halves(left)
    both = jnp.concatenate([high, low], axis=0)
    for start in range(0, high_ref.shape[1], strip):
        at = slice(start, start + strip)
        main = jnp.dot(both, high_ref[:, at], preferred_element_type=jnp.float32)
        rest = jnp.dot(high, low_ref[:, at], preferred_element_type=jnp.float32)
        yield at, main[:rows] + main[rows:] + rest


def dense_kernel(lists_hbm, blocks_hbm, high_ref, low_ref, lists_ref, blocks_ref, semaphores):
    count, size = blocks_ref.shape[0], blocks_ref.shape[-1]
    chunk = count // math.gcd(count, CHUNKS)
    copies = [pltpu.make_async_copy(lists_hbm.at[0, 0], lists_ref, semaphores.at[0])]
    for at, start in enumerate(range(0, count, chunk)):
        part = pl.ds(start, chunk)
        copies.append(
            pltpu.make_async_copy(
                blocks_hbm.at[0, 0, part], blocks_ref.at[part], semaphores.at[1 + at]
            )
        )
    for copy in copies:
        copy.start()
    high_ref[...] = jnp.zeros_like(high_ref)
    low_ref[...] = jnp.zeros_like(low_ref)
    copies[0].wait()
    for at, copy in enumerate(copies[1:]):
        copy.wait()

        @pl.loop(at * chunk, (at + 1) * chunk, unroll=UNROLL)
        def _(k):
            row = pl.ds(pl.multiple_of(lists_ref[0, k] * size, size), size)
            col = pl.ds(pl.multiple_of(lists_ref[1, k] * size, size), size)
            high_ref[row, col], low_ref[row, col] = halves(blocks_ref[k])


def transpose_kernel(high_ref, low_ref, high_t_ref, low_t_ref):
    for start in range(0, high_ref.shape[0], 128):
        at = slice(start, start + 128)
        high_t_ref[at, :] = high_ref[:, at].T
        low_t_ref[at, :] = low_ref[:, at].T


def summed(terms):
    total = terms[0][...]
    for term in terms[1:]:
        total = total + term[...]
    return total


def partner_order(n_off, n_row):
    offset, row = lax.axis_index("off"), lax.axis_index("row")
    ahead_first = offset >= 0
    for distance in range(1, n_off):
        parity = lax.rem(lax.div(row, math.gcd(distance, n_row)), 2)
        ahead_first = jnp.where(offset == distance, parity == 0, ahead_first)
    return ahead_first


def write_products(ahead_first, total, high_ref, low_ref, first_ref, second_ref):
    for at, value in product(total, high_ref, low_ref, 256):
        second_ref[:, at] = jnp.where(ahead_first, total[:, at], value)
        first_ref[:, at] = jnp.where(ahead_first, value, total[:, at])


def turn_kernel(groups, piece_ref, *outs):
    turned = piece_ref[...].T
    width = turned.shape[0] // groups
    for group, out in enumerate(outs):
        out[...] = turned[group * width : (group + 1) * width]


def first_kernel(n_off, n_row, *refs):
    pieces, (high_ref, low_ref) = refs[:n_off], refs[n_off : n_off + 2]
    vectors_ref, second_ref, first_ref = refs[-3:]
    rows = pieces[0].shape[1]
    for step, piece in enumerate(pieces):
        owner = lax.rem(lax.axis_index("off") - step + n_off, n_off)
        vectors_ref[:, pl.ds(pl.multiple_of(owner * rows, rows), rows)] = piece[...]
    write_products(
        partner_order(n_off, n_row),
        vectors_ref[...],
        high_ref,
        low_ref,
        first_ref,
        second_ref,
    )


def step_kernel(n_off, n_row, scale, has_older, keeps, *refs):
    total = scale * summed(refs[:n_off])
    if has_older:
        total = total - refs[n_off][...]
    if keeps:
        refs[-3][...] = total
    high_ref, low_ref = refs[n_off + has_older : n_off + has_older + 2]
    second_ref, first_ref = refs[-2:]
    write_products(
        partner_order(n_off, n_row), total, high_ref, low_ref, first_ref, second_ref
    )


def far_kernel(n_off, steps, *refs):
    own_second, second, own_first, first, high_ref, low_ref, *outs = refs
    offset = lax.axis_index("off")
    ahead_first = partner_order(n_off, lax.axis_size("row"))

    def received(own, if_ahead, if_not, at):
        value = jnp.where(ahead_first, if_ahead[:, at], if_not[:, at])
        return jnp.where(offset == 0, own[:, at], value)

    far = received(own_second, first, second, slice(None))
    for step, out in zip(steps, outs):
        rows = out.shape[1]
        strip = min(256, rows)
        base = 0 if step is None else lax.rem(offset + step, n_off) * rows
        for start in range(0, rows, strip):
            at = pl.ds(base + start, strip) if step is None else pl.ds(
                pl.multiple_of(base + start, strip), strip
            )
            [(_, value)] = product(far, high_ref.at[:, at], low_ref.at[:, at], strip)
            out[:, start : start + strip] = value + received(own_first, second, first, at)


def last_kernel(n_off, groups, *refs):
    out_ref = refs[-1]
    rows = out_ref.shape[0]
    at = pl.ds(pl.multiple_of(lax.axis_index("off") * rows, rows), rows)
    result = []
    for group in range(groups):
        total = summed(refs[group * n_off : (group + 1) * n_off])
        result.append(later_scale * total - refs[groups * n_off + group][:, at])
    out_ref[...] = jnp.concatenate(result, axis=0).T


def kernel_call(body, in_specs, shapes, scratch=(), flops=0):
    return pl.pallas_call(
        body,
        out_shape=shapes,
        in_specs=in_specs,
        out_specs=[VMEM] * len(shapes),
        scratch_shapes=list(scratch),
        compiler_params=pltpu.CompilerParams(vmem_limit_bytes=24 * 2**20),
        cost_estimate=pl.CostEstimate(flops=flops, bytes_accessed=0, transcendentals=0),
    )


def per_device(vectors, blocks, lists):
    n_off = lax.axis_size("off")
    n_row = lax.axis_size("row")
    piece_rows, width = vectors.shape
    tile_rows = piece_rows * n_off
    group_width = width // GROUPS

    def shifted(value, distance):
        return lax.ppermute(value, "off", [(d, (d + distance) % n_off) for d in range(n_off)])

    def swapped(value, ahead):
        route = []
        for i in range(n_row):
            for d in range(n_off):
                step = math.gcd(d, n_row) if d else 1
                assert n_row // step % 2 == 0
                forward = i // step % 2 == (1 - ahead if d else 0)
                partner = (i + (d or 1) * (1 if forward else -1)) % n_row
                route.append((i * n_off + d, partner * n_off + d))
        return [value, lax.ppermute(value, ("row", "off"), route)]

    f32 = lambda *shape: jax.ShapeDtypeStruct(shape, jnp.float32)
    bf16 = jax.ShapeDtypeStruct((tile_rows, tile_rows), jnp.bfloat16)
    group_shape = f32(group_width, tile_rows)
    piece_shape = f32(group_width, piece_rows)
    flops = 6 * group_width * tile_rows * tile_rows

    pieces = kernel_call(functools.partial(turn_kernel, GROUPS), [VMEM], [piece_shape] * GROUPS)(
        vectors
    )
    pieces = [[piece] + [shifted(piece, s) for s in range(1, n_off)] for piece in pieces]
    count = blocks.shape[2]
    high, low = kernel_call(
        dense_kernel,
        [HBM, HBM],
        [bf16] * 2,
        [
            pltpu.SMEM(lists.shape[2:], lists.dtype),
            pltpu.VMEM(blocks.shape[2:], blocks.dtype),
            pltpu.SemaphoreType.DMA((1 + math.gcd(count, CHUNKS),)),
        ],
    )(*(pltpu.with_memory_space_constraint(x, pltpu.HBM) for x in (lists, blocks)))
    high_t, low_t = kernel_call(transpose_kernel, [VMEM] * 2, [bf16] * 2, flops=flops)(high, low)

    older, newer = [None] * GROUPS, [None] * GROUPS
    totals = [None] * GROUPS
    for degree in range(DEGREE):
        scale = first_scale if degree == 1 else later_scale
        last = degree == DEGREE - 1
        seconds = []
        firsts = []
        for g in range(GROUPS):
            if degree == 0:
                body = functools.partial(first_kernel, n_off, n_row)
                terms = pieces[g]
            else:
                body = functools.partial(
                    step_kernel, n_off, n_row, scale, int(degree > 1), not last
                )
                terms = [totals[g]] + [shifted(totals[g], s) for s in range(1, n_off)]
                terms += [older[g]] if degree > 1 else []
            kept = [] if last else [group_shape]
            *kept, second, first = kernel_call(
                body, [VMEM] * (len(terms) + 2), kept + [group_shape] * 2, flops=flops
            )(*terms, high, low)
            older[g], newer[g] = newer[g], kept[0] if kept else None
            seconds.append(swapped(second, 0))
            firsts.append(swapped(first, 1))
        for g in range(GROUPS):

            def far_terms(*steps):
                shape = group_shape if steps[0] is None else piece_shape
                return kernel_call(
                    functools.partial(far_kernel, n_off, steps),
                    [VMEM] * 6,
                    [shape] * len(steps),
                    flops=flops,
                )(*seconds[g], *firsts[g], high_t, low_t)

            if last:
                totals[g] = far_terms(*range(1, n_off))
                totals[g] = far_terms(0) + totals[g]
            else:
                [totals[g]] = far_terms(None)
    terms = []
    for g in range(GROUPS):
        terms.append(totals[g][0])
        terms.extend(shifted(totals[g][s], s) for s in range(1, n_off))
    [result] = kernel_call(
        functools.partial(last_kernel, n_off, GROUPS),
        [VMEM] * (GROUPS * (n_off + 1)),
        [f32(piece_rows, width)],
    )(*terms, *older)
    return result


def solution(mesh):
    in_specs = (
        P(("row", "off"), None),
        P("row", "off", None, None, None),
        P("row", "off", None, None),
    )
    out_specs = P(("row", "off"), None)
    return jax.shard_map(
        per_device, mesh=mesh, in_specs=in_specs, out_specs=out_specs, check_vma=False
    )
```
